32 devices in a mesh: groups: 2 (over y), attn: 4 (over x, core), expert: 4 (over z).
Axes of the slice: x: 2, y: 2, z: 4, core: 2. Of those that a mesh axis runs over, the one named last changes fastest.
Arguments:
- tokens: bfloat16 [1024, 4096], P(('groups', 'attn')), parts along dimension 0, may hold values from -6 to 6
- norm_gain: float32 [4096], replicated, may hold values from 0.1 to 1.9
- query_weight: bfloat16 [4096, 4096], P('attn', 'expert'), may hold values from -0.09375 to 0.09375
- key_weight: bfloat16 [4096, 1024], P('attn', 'expert'), may hold values from -0.09375 to 0.09375
- value_weight: bfloat16 [4096, 1024], P('attn', 'expert'), may hold values from -0.09375 to 0.09375
- out_weight: bfloat16 [4096, 4096], P('attn', 'expert'), may hold values from -0.09375 to 0.09375
- cache_key: bfloat16 [8, 2048, 1024], P(('groups', 'attn'), None, 'expert'), parts along dimension 0, may hold values from -240 to 240
- cache_value: bfloat16 [8, 2048, 1024], P(('groups', 'attn'), None, 'expert'), parts along dimension 0, may hold values from -24 to 24
- block_table: int32 [8, 8], P(('groups', 'attn')), parts along dimension 0, may hold values from 0 to 15
- block_count: int32 [8], P(('groups', 'attn')), parts along dimension 0, may hold values from 1 to 8, 24 in all
- expert_ids: int32 [1024, 2], P(('groups', 'attn')), parts along dimension 0, may hold values from 0 to 3, all different within a row; in each aligned block of 128 rows (0 to 127, 128 to 255, ...) at most 96 rows name the same one
- gate_weights: float32 [1024, 2], P(('groups', 'attn')), parts along dimension 0, may hold values from 1 to 3
- post_gain: float32 [4096], replicated, may hold values from 0.1 to 1.9
- expert_gate: bfloat16 [4, 4096, 6400], P('expert', None, 'attn'), may hold values from -0.09375 to 0.09375
- expert_up: bfloat16 [4, 4096, 6400], P('expert', None, 'attn'), may hold values from -0.09375 to 0.09375
- expert_down: bfloat16 [4, 6400, 4096], P('expert', 'attn'), may hold values from -0.15625 to 0.15625
Outputs:
- mixed: bfloat16 [1024, 4096], P(('groups', 'attn'), 'expert'), parts along dimension 0
The draws below stay inside these ranges and needn't reach their ends.
There are 2 independent parts, one for each index of `groups`. The reference program is written for one: setup_inputs(seed, part) draws one part's arguments, and reference() takes and returns one part's arrays. A program takes and returns all parts, laid end to end along the dimension named above; an argument that names none is the same for every part. Nothing has to cross between parts.
Inputs may be any that keep to these rules, and one draw needn't show every extreme that they name: `expert_ids`: in each aligned block of 128 tokens (one sequence) no expert is named more than 96 times; the two ids of a token differ. `block_count`: the counts of one part sum to 24.
All inputs are finite; a program needn't handle non-finite values. No bound on the sum of `block_count` on one device may be relied on, other than what follows from the above.
Results may differ from the reference program's by a relative error of at most 0.02.
Values may be sent and summed in bfloat16 or wider, within the bound.
A program may use at most 128 MiB of HBM per device.

```python
import math
from functools import partial
import jax
import jax.numpy as jnp
import numpy as np
from jax import lax

D = 4096
HEADS = 32
KVH = 8
HD = 128
FF = 6400
ROWS = 128
CACHE_BLOCKS = 16
NSEL = 8
BLK = 128
EXPERTS = 4
SEQS = 4
TOKENS = 512
CAP = 96
N_ATTN = 4


def draw_cache_key(key, part):
    full_shape = (SEQS, CACHE_BLOCKS, BLK, KVH, HD)
    base_values = jnp.clip(jax.random.normal(jax.random.fold_in(key, 17), full_shape, jnp.float32), -6.0, 6.0)
    return base_values.reshape(SEQS, CACHE_BLOCKS * BLK, KVH * HD).astype(jnp.bfloat16)


def plant(drawn, key, least, high):
    shape = drawn.shape
    spot = [jax.random.randint(jax.random.fold_in(key, axis), (), 0, shape[axis]) for axis in range(len(shape))]
    drawn = drawn.at[tuple(spot)].set(least)
    longest = shape.index(max(shape))
    spot[longest] = (spot[longest] + 1) % shape[longest]
    return drawn.at[tuple(spot)].set(high)


def steps_of(stream_key, extent, pieces, least, high):
    def one(dim, shards_of):
        heights = jax.random.uniform(jax.random.fold_in(jax.random.fold_in(stream_key, 6), dim), (shards_of,), jnp.float32, least / len(pieces), high / len(pieces))
        return jnp.repeat(jnp.exp(heights), extent[dim] // shards_of).reshape((-1,) + (1,) * (len(extent) - dim - 1))

    gain = one(*pieces[0])
    for cut in pieces[1:]:
        gain = gain * one(*cut)
    return gain


def split_up(number_of, total, most, lean):
    portions = [(1 << 20) // math.isqrt(standing ** lean) + 1 for standing in range(2, number_of + 1)]
    spare, given = total - most - (number_of - 1), [1] * (number_of - 1)
    while spare > 0:
        movable = [i for i in range(number_of - 1) if given[i] < most]
        pool, remaining = sum([portions[i] for i in movable]), spare
        for i in movable:
            addition = min(most - given[i], max(1, remaining * portions[i] // pool), spare)
            given[i] = given[i] + addition
            spare = spare - addition
    return np.array([most] + given)


def uneven_parts(stream_key, number_of, total, limit, lean):
    if number_of == 2:
        one = jax.random.randint(stream_key, (), max(1, total - limit), min(limit, total - 1) + 1)
        return jnp.stack([one, total - one])
    sizes = jnp.asarray(split_up(number_of, total, limit, lean), jnp.int32)
    twos = (number_of - 1) // 2
    giver, sink = sizes[1:1 + 2 * twos:2], sizes[2:2 + 2 * twos:2]
    slack = jnp.minimum(giver - 1, limit - sink)
    shifted = jax.random.randint(jax.random.fold_in(stream_key, 1), (twos,), 0, 1 << 20) % (slack + 1)
    sizes = sizes.at[1:1 + 2 * twos:2].set(giver - shifted).at[2:2 + 2 * twos:2].set(sink + shifted)
    return sizes[jax.random.permutation(jax.random.fold_in(stream_key, 2), number_of)]


def shared_out(stream_key, own, number, rows, number_of, top, limit, lean):
    order = jax.random.permutation(stream_key, number_of)
    crowded, ordinary = load_shares(number_of, rows * top, limit, lean, True), load_shares(number_of, rows * top, limit, lean, False)
    places = jnp.arange(number_of)

    def named(lengths, turn):
        used = int((lengths > 0).sum())
        fixed = max(1, used // 4)
        passed = fixed + (places - fixed + turn * (used - fixed)) % max(1, number_of - fixed)
        return jnp.zeros((number_of,), jnp.int32).at[order[jnp.where(places < fixed, places, passed)]].set(jnp.asarray(lengths, jnp.int32))

    lengths = jnp.where(number % 4 == 0, named(crowded, number // 4), named(ordinary, number - number // 4 - 1))
    mixed = jax.random.permutation(jax.random.fold_in(own, 3), number_of)
    donor, receiver = mixed[0:number_of // 2 * 2:2], mixed[1:number_of // 2 * 2:2]
    slack = jnp.minimum(lengths[donor] - 1, limit - lengths[receiver]) // 2
    slack = jnp.where((donor == order[0]) | (receiver == order[0]) | (lengths[receiver] == 0), 0, jnp.maximum(slack, 0))
    passed = jax.random.randint(jax.random.fold_in(own, 4), (number_of // 2,), 0, 1 << 20) % (slack + 1)
    lengths = lengths.at[donor].add(-passed).at[receiver].add(passed)
    labels = jnp.searchsorted(jnp.cumsum(lengths), jnp.arange(rows * top), side="right").astype(jnp.int32)
    table = labels.reshape(top, rows).T
    table = table[jax.random.permutation(jax.random.fold_in(own, 1), rows)]
    turn = jax.random.randint(jax.random.fold_in(own, 2), (rows, 1), 0, top)
    return jnp.take_along_axis(table, (jnp.arange(top)[None, :] + turn) % top, axis=1)


def load_shares(amount, total, most, slope, full):
    portions = [(1 << 20) // math.isqrt(rank ** slope) + 1 for rank in range(1, amount + 1)]
    largest = most if full else min(most, max(-(-total // amount), total * portions[0] // sum(portions)))
    least = 1 if total - largest >= amount - 1 else 0
    counts, rest = [largest] + [least] * (amount - 1), total - largest - least * (amount - 1)
    while rest > 0:
        free = [i for i in range(1, amount) if counts[i] < largest] or [i for i in range(1, amount) if counts[i] < most]
        mass, remaining = sum([portions[i] for i in free]), rest
        for i in free:
            addition = min(most - counts[i], max(1, remaining * portions[i] // mass), rest)
            counts[i] = counts[i] + addition
            rest = rest - addition
    return np.array(counts)


def scatter_about(rng, shape, scale, reach, shards=(), kind=jnp.bfloat16):
    array = scale * jax.random.normal(rng, shape, jnp.float32)
    if shards:
        array = array * steps_of(rng, shape, shards, -0.22, 0.18)
    return jnp.clip(array, -reach, reach).astype(kind)


def setup_inputs(seed: int = 0, part: int = 0) -> dict:
    arg_keys = jax.random.split(jax.random.key(seed), 17)
    own_keys = jax.random.split(jax.random.fold_in(arg_keys[16], part), 17)
    tokens = scatter_about(own_keys[0], (TOKENS, D), 1.0, 6.0, ((0, 4),))
    norm_gain = jnp.clip(1.0 + 0.18 * jax.random.normal(arg_keys[1], (D,), jnp.float32), 0.1, 1.9)
    query_weight = scatter_about(arg_keys[2], (D, HEADS * HD), D ** -0.5, 0.09375, ((0, 4), (1, 4)))
    key_weight = scatter_about(arg_keys[3], (D, KVH * HD), D ** -0.5, 0.09375, ((0, 4), (1, 4)))
    value_weight = scatter_about(arg_keys[4], (D, KVH * HD), D ** -0.5, 0.09375, ((0, 4), (1, 4)))
    out_weight = scatter_about(arg_keys[5], (D, HEADS * HD), (HEADS * HD) ** -0.5, 0.09375, ((0, 4), (1, 4)))
    cache_key = draw_cache_key(jax.random.fold_in(jax.random.fold_in(arg_keys[16], part), 71), part)
    cache_value = scatter_about(own_keys[7], (SEQS, CACHE_BLOCKS * BLK, KVH * HD), 4.0, 24.0, ((0, 4), (2, 4)))
    block_table = plant(jax.random.randint(own_keys[8], (SEQS, NSEL), 0, CACHE_BLOCKS), jax.random.fold_in(own_keys[8], 1), 0, CACHE_BLOCKS - 1).astype(jnp.int32)
    block_count = uneven_parts(own_keys[9], SEQS, N_ATTN * NSEL * 3 // 4, NSEL, 2).astype(jnp.int32)
    expert_ids_keys = jax.random.split(jax.random.fold_in(own_keys[10], 1), TOKENS // ROWS)
    expert_ids_turns = jax.random.permutation(jax.random.fold_in(own_keys[10], 3), TOKENS // ROWS)
    expert_ids = jax.vmap(lambda own, number: shared_out(jax.random.fold_in(own_keys[10], 2), own, number, ROWS, EXPERTS, 2, CAP, 2))(expert_ids_keys, expert_ids_turns).reshape((TOKENS, 2))
    gate_weights = jnp.clip(1.0 + 2.0 * jax.random.uniform(own_keys[11], (TOKENS, 2), jnp.float32) ** steps_of(own_keys[11], (TOKENS, 2), ((0, 4),), -0.2, 0.2), 1.0, 3.0)
    post_gain = jnp.clip(1.0 + 0.18 * jax.random.normal(arg_keys[12], (D,), jnp.float32), 0.1, 1.9)
    expert_gate = scatter_about(arg_keys[13], (EXPERTS, D, FF), D ** -0.5, 0.09375, ((0, 4), (2, 4)))
    expert_up = scatter_about(arg_keys[14], (EXPERTS, D, FF), D ** -0.5, 0.09375, ((0, 4), (2, 4)))
    expert_down = scatter_about(arg_keys[15], (EXPERTS, FF, D), (FF // 4) ** -0.5, 0.15625, ((0, 4), (1, 4)))
    return {"tokens": tokens, "norm_gain": norm_gain, "query_weight": query_weight, "key_weight": key_weight, "value_weight": value_weight, "out_weight": out_weight, "cache_key": cache_key, "cache_value": cache_value, "block_table": block_table, "block_count": block_count, "expert_ids": expert_ids, "gate_weights": gate_weights, "post_gain": post_gain, "expert_gate": expert_gate, "expert_up": expert_up, "expert_down": expert_down}


epsilon = 1e-05
rope_base = 10000.0

def layer_norm(values, gain_vector):
    center = lax.optimization_barrier(jnp.mean(values, axis=-1, keepdims=True))
    spread = lax.optimization_barrier(jnp.mean(jnp.square(values - center), axis=-1, keepdims=True))
    return (values - center) * lax.rsqrt(spread + epsilon) * gain_vector

def rotate(values, positions, head_size):
    row_count = values.shape[0]
    head_count = values.shape[1] // head_size
    half_size = head_size // 2
    frequency = jnp.exp(jnp.arange(half_size, dtype=jnp.float32) * (-2.0 * math.log(rope_base) / head_size))
    angle_table = positions[:, None] * frequency[None, :]
    cosine = jnp.cos(angle_table)[:, None, :]
    sine_part = jnp.sin(angle_table)[:, None, :]
    split_heads = values.reshape(row_count, head_count, head_size)
    first_half = split_heads[..., :half_size]
    second_half = split_heads[..., half_size:]
    turned = jnp.concatenate([first_half * cosine - second_half * sine_part, second_half * cosine + first_half * sine_part], axis=-1)
    return turned.reshape(row_count, head_count * head_size)

def pair_slots(expert_ids, expert_total):
    flat_ids = expert_ids.reshape(-1)
    onehot = (flat_ids[:, None] == jnp.arange(expert_total, dtype=jnp.int32)[None, :]).astype(jnp.int32)
    earlier = jnp.cumsum(onehot, axis=0) - onehot
    return lax.optimization_barrier(jnp.sum(onehot * earlier, axis=1)).reshape(expert_ids.shape)

def attend(inputs):
    query_rows, fresh_keys, fresh_values, cache_keys, cache_values, block_list, live_blocks = inputs
    row_count = query_rows.shape[0]
    key_heads = fresh_keys.shape[1] // HD
    group_size = query_rows.shape[1] // fresh_keys.shape[1]
    picked_keys = jnp.take(cache_keys.reshape(CACHE_BLOCKS, BLK, -1), block_list, axis=0).reshape(NSEL * BLK, key_heads, HD)
    picked_values = jnp.take(cache_values.reshape(CACHE_BLOCKS, BLK, -1), block_list, axis=0).reshape(NSEL * BLK, key_heads, HD)
    all_keys = jnp.concatenate([picked_keys, fresh_keys.reshape(row_count, key_heads, HD)], axis=0).astype(jnp.float32)
    all_values = jnp.concatenate([picked_values, fresh_values.reshape(row_count, key_heads, HD)], axis=0).astype(jnp.float32)
    queries = query_rows.reshape(row_count, key_heads, group_size, HD).astype(jnp.float32)
    score_scale = 1.0 / math.sqrt(HD)
    scores = jnp.einsum('rkgd,nkd->kgrn', queries, all_keys) * score_scale
    live_keys = jnp.arange(NSEL * BLK, dtype=jnp.int32) // BLK < live_blocks
    row_range = jnp.arange(row_count, dtype=jnp.int32)
    causal = row_range[:, None] >= row_range[None, :]
    allowed = jnp.concatenate([jnp.broadcast_to(live_keys[None, :], (row_count, NSEL * BLK)), causal], axis=1)
    scores = jnp.where(allowed, scores, -jnp.inf)
    largest = lax.optimization_barrier(jnp.max(scores, axis=-1, keepdims=True))
    exponent = jnp.exp(scores - largest)
    weights = (exponent / lax.optimization_barrier(jnp.sum(exponent, axis=-1, keepdims=True))).astype(jnp.bfloat16)
    context = jnp.einsum('kgrn,nkd->rkgd', weights.astype(jnp.float32), all_values)
    return context.reshape(row_count, -1).astype(jnp.bfloat16)

def reference(tokens, norm_gain, query_weight, key_weight, value_weight, out_weight, cache_key, cache_value, block_table, block_count, expert_ids, gate_weights, post_gain, expert_gate, expert_up, expert_down):
    normed = layer_norm(tokens.astype(jnp.float32), norm_gain).astype(jnp.bfloat16)
    normed_wide = normed.astype(jnp.float32)
    row_range = jnp.arange(ROWS, dtype=jnp.int32)
    positions = (block_count[:, None] * BLK + row_range[None, :]).reshape(-1).astype(jnp.float32)
    query = rotate(jnp.dot(normed_wide, query_weight.astype(jnp.float32), preferred_element_type=jnp.float32), positions, HD).astype(jnp.bfloat16)
    key_new = rotate(jnp.dot(normed_wide, key_weight.astype(jnp.float32), preferred_element_type=jnp.float32), positions, HD).astype(jnp.bfloat16)
    value_new = jnp.dot(normed_wide, value_weight.astype(jnp.float32), preferred_element_type=jnp.float32).astype(jnp.bfloat16)
    context = lax.map(attend, (query.reshape(SEQS, ROWS, -1), key_new.reshape(SEQS, ROWS, -1), value_new.reshape(SEQS, ROWS, -1), cache_key, cache_value, block_table, block_count))
    context = context.reshape(TOKENS, -1)
    attended = jnp.dot(context.astype(jnp.float32), out_weight.astype(jnp.float32).T, preferred_element_type=jnp.float32)
    state = (tokens.astype(jnp.float32) + attended).astype(jnp.bfloat16)
    post_normed = layer_norm(state.astype(jnp.float32), post_gain).astype(jnp.bfloat16)
    slots = jax.vmap(partial(pair_slots, expert_total=EXPERTS))(expert_ids.reshape(SEQS, ROWS, 2)).reshape(TOKENS, 2)
    sequence_of = jnp.arange(TOKENS, dtype=jnp.int32) // ROWS
    mixture = jnp.zeros((TOKENS, D), jnp.float32)
    unit_group = FF // N_ATTN
    for expert in range(EXPERTS):
        target = jnp.where(expert_ids == expert, sequence_of[:, None] * CAP + slots, SEQS * CAP).astype(jnp.int32)
        buffer = jnp.zeros((SEQS * CAP, D), jnp.bfloat16)
        for pick in range(2):
            buffer = buffer.at[target[:, pick]].set(post_normed, mode='drop')
        buffer_wide = buffer.astype(jnp.float32)
        gated = jnp.dot(buffer_wide, expert_gate[expert].astype(jnp.float32), preferred_element_type=jnp.float32)
        lifted = jnp.dot(buffer_wide, expert_up[expert].astype(jnp.float32), preferred_element_type=jnp.float32)
        activated = lax.optimization_barrier((jax.nn.silu(gated) * lifted).astype(jnp.bfloat16)).astype(jnp.float32)
        down_wide = expert_down[expert].astype(jnp.float32)
        summed = jnp.zeros((SEQS * CAP, D), jnp.float32)
        for group_index in range(N_ATTN):
            lower = group_index * unit_group
            partial_out = jnp.dot(activated[:, lower:lower + unit_group], down_wide[lower:lower + unit_group], preferred_element_type=jnp.float32)
            summed = summed + lax.optimization_barrier(partial_out.astype(jnp.bfloat16)).astype(jnp.float32)
        expert_out = lax.optimization_barrier(summed.astype(jnp.bfloat16)).astype(jnp.float32)
        for pick in range(2):
            gathered = jnp.take(expert_out, jnp.minimum(target[:, pick], SEQS * CAP - 1), axis=0)
            chosen = (expert_ids[:, pick] == expert).astype(jnp.float32)
            mixture = mixture + gathered * (chosen * gate_weights[:, pick])[:, None]
    return (state.astype(jnp.float32) + mixture).astype(jnp.bfloat16)
```

```python
import functools
import math

import jax
import jax.numpy as jnp
from jax import lax
from jax.experimental import pallas as pl
from jax.experimental.pallas import tpu as pltpu
from jax.sharding import PartitionSpec as P

HD = 128
BLK = 128
TILE = 256
LAG = 4
TRANSPOSED = (((1,), (1,)), ((), ()))
MESH = pl.DeviceIdType.MESH


epsilon = 1e-05
rope_base = 10000.0


def pair_slots(expert_ids, expert_total):
    flat_ids = expert_ids.reshape(-1)
    onehot = (flat_ids[:, None] == jnp.arange(expert_total, dtype=jnp.int32)[None, :]).astype(
        jnp.int32
    )
    earlier = jnp.cumsum(onehot, axis=0) - onehot
    return jnp.sum(onehot * earlier, axis=1).reshape(expert_ids.shape)


def moe_kernel(
    chips,
    depth,
    buffer_ref,
    gate_ref,
    up_ref,
    down_ref,
    picks_ref,
    weights_ref,
    out_ref,
    gate_all,
    up_all,
    down_all,
    piece,
    activated,
    partial,
    keep,
    pair_send,
    pair_recv,
    chip_send,
    chip_recv,
    mine,
    mix_send,
    mix_recv,
    load_sem,
    gather_send,
    forward_send,
    gather_recv,
    pair_send_sem,
    pair_recv_sem,
    chip_send_sem,
    chip_recv_sem,
    mix_send_sem,
    mix_recv_sem,
):
    me = lax.axis_index("attn")
    expert = lax.axis_index("expert")
    chip = me // 2
    core = me % 2
    partner = me + 1 - 2 * core
    capacity = buffer_ref.shape[0]
    hidden = activated.shape[1]
    steps = pair_send.shape[0]
    width = partial.shape[1]
    per_owner = steps // depth
    loads = [
        pltpu.make_async_copy(source.at[0], target, load_sem.at[i])
        for i, (source, target) in enumerate(
            [(gate_ref, gate_all), (up_ref, up_all), (down_ref, down_all)]
        )
    ]
    for load in loads:
        load.start()

    def other_chip(k):
        return lax.rem(chip + k, chips)

    def other_expert(k):
        return lax.rem(expert + k, depth)

    barrier = pltpu.get_barrier_semaphore()
    pl.semaphore_signal(barrier, inc=1, device_id={"attn": partner}, device_id_type=MESH)
    for k in range(1, chips):
        pl.semaphore_signal(
            barrier, inc=1, device_id={"attn": other_chip(k) * 2 + core}, device_id_type=MESH
        )
    for k in range(1, depth):
        pl.semaphore_signal(
            barrier, inc=1, device_id={"expert": other_expert(k)}, device_id_type=MESH
        )
    pl.semaphore_wait(barrier, chips + depth - 1)

    def seq_rows(seq, count=1):
        return pl.ds(pl.multiple_of(seq * capacity, 16), count * capacity)

    def send(source, target, send_sem, recv_sem, where):
        return pltpu.make_async_remote_copy(
            src_ref=source,
            dst_ref=target,
            send_sem=send_sem,
            recv_sem=recv_sem,
            device_id=where,
            device_id_type=MESH,
        )

    def gather_copy(k):
        where = {"attn": partner} if k == 0 else {"attn": other_chip(k) * 2 + core}
        return send(
            buffer_ref, piece.at[seq_rows(me)], gather_send.at[k], gather_recv.at[me], where
        )

    def forward_copy(k):
        seq = other_chip(k) * 2 + core
        return send(
            piece.at[seq_rows(seq)],
            piece.at[seq_rows(seq)],
            forward_send.at[k],
            gather_recv.at[seq],
            {"attn": partner},
        )

    def arrival(seq):
        return send(
            buffer_ref,
            piece.at[seq_rows(seq)],
            gather_send.at[0],
            gather_recv.at[seq],
            {"attn": partner},
        )

    for k in range(1, chips):
        gather_copy(k).start()
    gather_copy(0).start()
    piece[seq_rows(me), :] = buffer_ref[...]

    def hidden_tile(rows, start, size):
        values = piece[rows, :]
        columns = pl.ds(start, size)
        gated = lax.dot_general(
            values, gate_all[columns, :], TRANSPOSED, preferred_element_type=jnp.float32
        )
        lifted = lax.dot_general(
            values, up_all[columns, :], TRANSPOSED, preferred_element_type=jnp.float32
        )
        activated[rows, columns] = (jax.nn.silu(gated) * lifted).astype(jnp.bfloat16)

    for k in range(chips):
        if k == 0:
            arrival(partner).wait_recv()
            loads[0].wait()
            loads[1].wait()
        else:
            seq = other_chip(k) * 2 + core
            arrival(seq).wait_recv()
            forward_copy(k).start()
            arrival(other_chip(k) * 2 + 1 - core).wait_recv()
        rows = seq_rows(other_chip(k) * 2, 2)
        full = hidden // TILE

        def tile_body(tile, carry):
            hidden_tile(rows, pl.multiple_of(tile * TILE, TILE), TILE)
            return carry

        lax.fori_loop(0, full, tile_body, 0)
        if hidden % TILE:
            hidden_tile(rows, full * TILE, hidden % TILE)
    loads[2].wait()

    def owner_of(step):
        return lax.rem(expert + 1 + step // per_owner, depth)

    def pair_copy(step):
        return send(
            pair_send.at[step],
            pair_recv.at[step],
            pair_send_sem.at[step],
            pair_recv_sem.at[step],
            {"attn": partner},
        )

    def chip_copy(step, k):
        return send(
            chip_send.at[step, k],
            chip_recv.at[step, chip],
            chip_send_sem.at[step, k],
            chip_recv_sem.at[step, chip],
            {"attn": other_chip(k) * 2 + core},
        )

    def chip_arrival(step, k):
        return send(
            chip_send.at[step, k],
            chip_recv.at[step, other_chip(k)],
            chip_send_sem.at[step, k],
            chip_recv_sem.at[step, other_chip(k)],
            {"attn": other_chip(k) * 2 + core},
        )

    def mix_copy(step):
        return send(
            mix_send.at[step],
            mix_recv.at[expert, lax.rem(step, per_owner)],
            mix_send_sem.at[step],
            mix_recv_sem.at[expert, lax.rem(step, per_owner)],
            {"expert": owner_of(step)},
        )

    def mix_arrival(source, part):
        return send(
            mix_send.at[0],
            mix_recv.at[source, part],
            mix_send_sem.at[0],
            mix_recv_sem.at[source, part],
            {"expert": source},
        )

    def project(step):
        columns = pl.ds(
            pl.multiple_of((owner_of(step) * per_owner + lax.rem(step, per_owner)) * width, width),
            width,
        )
        partial[...] = jnp.dot(
            activated[...], down_all[:, columns], preferred_element_type=jnp.float32
        )
        for k in range(chips):
            keep[lax.rem(step, 2), k] = partial[seq_rows(other_chip(k) * 2 + core), :]
            pair_send[step, other_chip(k)] = partial[
                seq_rows(other_chip(k) * 2 + 1 - core), :
            ].astype(jnp.bfloat16)
        pair_copy(step).start()

    def pair_sum(step):
        pair_copy(step).wait_recv()
        for k in range(chips):
            both = keep[lax.rem(step, 2), k] + pair_recv[step, other_chip(k)].astype(jnp.float32)
            if k == 0:
                mine[step] = both
            else:
                chip_send[step, k] = both.astype(jnp.bfloat16)
                chip_copy(step, k).start()

    def combine(step):
        total = mine[step]
        for k in range(1, chips):
            chip_arrival(step, k).wait_recv()
            total = total + chip_recv[step, other_chip(k)].astype(jnp.float32)
        expert_out = total.astype(jnp.bfloat16)
        mixture = weights_ref[:, 0:1] * jnp.dot(
            picks_ref[0], expert_out, preferred_element_type=jnp.float32
        ) + weights_ref[:, 1:2] * jnp.dot(
            picks_ref[1], expert_out, preferred_element_type=jnp.float32
        )
        part = lax.rem(step, per_owner)

        @pl.when(step < steps - per_owner)
        def _():
            mix_send[step] = mixture.astype(jnp.bfloat16)
            mix_copy(step).start()

        @pl.when(step >= steps - per_owner)
        def _():
            out_ref[part] = mixture

    def step_body(step, carry):
        @pl.when(step < steps)
        def _():
            project(step)

        @pl.when((step >= 1) & (step <= steps))
        def _():
            pair_sum(step - 1)

        @pl.when(step >= LAG)
        def _():
            combine(step - LAG)

        return carry

    lax.fori_loop(0, steps + LAG, step_body, 0)

    for part in range(per_owner):
        total = out_ref[part]
        for k in range(1, depth):
            mix_arrival(other_expert(k), part).wait_recv()
            total = total + mix_recv[other_expert(k), part].astype(jnp.float32)
        out_ref[part] = total

    for k in range(chips):
        gather_copy(k).wait_send()
    for k in range(1, chips):
        forward_copy(k).wait_send()
    def finish(step, carry):
        pair_copy(step).wait_send()
        for k in range(1, chips):
            chip_copy(step, k).wait_send()

        @pl.when(step < steps - per_owner)
        def _():
            mix_copy(step).wait_send()

        return carry

    lax.fori_loop(0, steps, finish, 0)


def expert_layer(buffer, gate, up, down, picks, weights):
    n = lax.axis_size("attn")
    depth = lax.axis_size("expert")
    chips = n // 2
    capacity, model_width = buffer.shape
    hidden = gate.shape[2]
    row_count = weights.shape[0]
    share = model_width // depth
    width = math.gcd(share, 512)
    per_owner = share // width
    steps = model_width // width
    vmem = pl.BlockSpec(memory_space=pltpu.VMEM)
    anywhere = pl.BlockSpec(memory_space=pl.ANY)
    dma = pltpu.SemaphoreType.DMA
    out = pl.pallas_call(
        functools.partial(moe_kernel, chips, depth),
        out_shape=jax.ShapeDtypeStruct((per_owner, row_count, width), jnp.float32),
        in_specs=[vmem, anywhere, anywhere, anywhere, vmem, vmem],
        out_specs=vmem,
        scratch_shapes=[
            pltpu.VMEM((hidden, model_width), jnp.bfloat16),
            pltpu.VMEM((hidden, model_width), jnp.bfloat16),
            pltpu.VMEM((hidden, model_width), jnp.bfloat16),
            pltpu.VMEM((n * capacity, model_width), jnp.bfloat16),
            pltpu.VMEM((n * capacity, hidden), jnp.bfloat16),
            pltpu.VMEM((n * capacity, width), jnp.float32),
            pltpu.VMEM((2, chips, capacity, width), jnp.float32),
            pltpu.VMEM((steps, chips, capacity, width), jnp.bfloat16),
            pltpu.VMEM((steps, chips, capacity, width), jnp.bfloat16),
            pltpu.VMEM((steps, chips, capacity, width), jnp.bfloat16),
            pltpu.VMEM((steps, chips, capacity, width), jnp.bfloat16),
            pltpu.VMEM((steps, capacity, width), jnp.float32),
            pltpu.VMEM((steps, row_count, width), jnp.bfloat16),
            pltpu.VMEM((depth, per_owner, row_count, width), jnp.bfloat16),
            dma((3,)),
            dma((chips,)),
            dma((chips,)),
            dma((n,)),
            dma((steps,)),
            dma((steps,)),
            dma((steps, chips)),
            dma((steps, chips)),
            dma((steps,)),
            dma((depth, per_owner)),
        ],
        compiler_params=pltpu.CompilerParams(
            collective_id=0, has_side_effects=True, vmem_limit_bytes=63 * 1024 * 1024
        ),
        cost_estimate=pl.CostEstimate(
            flops=6 * n * capacity * model_width * hidden,
            bytes_accessed=6 * model_width * hidden,
            transcendentals=n * capacity * hidden,
        ),
    )(buffer, gate.swapaxes(1, 2), up.swapaxes(1, 2), down, picks, weights)
    return out.transpose(1, 0, 2).reshape(row_count, share)


def listed_kernel(table_ref, cache_key_ref, cache_value_ref, keys_ref, values_ref, sems):
    copies = []
    for j in range(table_ref.shape[1]):
        source = pl.ds(pl.multiple_of(table_ref[0, j] * BLK, BLK), BLK)
        target = pl.ds(j * BLK, BLK)
        for i, (cache, listed) in enumerate(
            [(cache_key_ref, keys_ref), (cache_value_ref, values_ref)]
        ):
            copies.append(
                pltpu.make_async_copy(cache.at[0, source], listed.at[target], sems.at[i, j])
            )
    for copy in copies:
        copy.start()
    for copy in copies:
        copy.wait()


def listed_blocks(block_table, cache_key, cache_value):
    listed = block_table.shape[1]
    shape = jax.ShapeDtypeStruct((listed * BLK, cache_key.shape[2]), cache_key.dtype)
    vmem = pl.BlockSpec(memory_space=pltpu.VMEM)
    anywhere = pl.BlockSpec(memory_space=pl.ANY)
    return pl.pallas_call(
        listed_kernel,
        out_shape=(shape, shape),
        in_specs=[pl.BlockSpec(memory_space=pltpu.SMEM), anywhere, anywhere],
        out_specs=(vmem, vmem),
        scratch_shapes=[pltpu.SemaphoreType.DMA((2, listed))],
    )(block_table, cache_key, cache_value)


def attention_kernel(
    chips,
    depth,
    tokens_ref,
    gain_ref,
    cosine_ref,
    sine_ref,
    bias_ref,
    post_gain_ref,
    dispatch_ref,
    query_weight_ref,
    key_weight_ref,
    value_weight_ref,
    cache_key_ref,
    cache_value_ref,
    out_weight_ref,
    buffer_ref,
    state_ref,
    query_all,
    key_all,
    value_all,
    cache_keys,
    cache_values,
    out_all,
    normed,
    pieces,
    partial,
    keep,
    pair_send,
    pair_recv,
    chip_send,
    chip_recv,
    projected,
    scores,
    contexts,
    head_sums,
    line_send,
    from_left,
    from_right,
    seq_send,
    seq_recv,
    states,
    post,
    load_sem,
    piece_send,
    piece_recv,
    pair_send_sem,
    pair_recv_sem,
    chip_send_sem,
    chip_recv_sem,
    gather_send,
    forward_send,
    gather_recv,
    line_send_sem,
    left_sem,
    right_sem,
    seq_send_sem,
    seq_recv_sem,
    state_right,
    state_left,
    state_recv,
):
    me = lax.axis_index("attn")
    expert = lax.axis_index("expert")
    n = 2 * chips
    chip = me // 2
    core = me % 2
    partner = me + 1 - 2 * core
    row_count, model_width = tokens_ref.shape
    block = model_width // n
    query_columns = query_all.shape[1]
    key_columns = key_all.shape[1]
    part_rows = row_count // depth
    loads = [
        pltpu.make_async_copy(source, target, load_sem.at[i])
        for i, (source, target) in enumerate(
            [
                (query_weight_ref, query_all),
                (key_weight_ref, key_all),
                (value_weight_ref, value_all),
                (cache_key_ref, cache_keys),
                (cache_value_ref, cache_values),
                (out_weight_ref, out_all),
            ]
        )
    ]
    for load in loads:
        load.start()

    def other_chip(k):
        return lax.rem(chip + k, chips)

    def send(source, target, send_sem, recv_sem, where):
        return pltpu.make_async_remote_copy(
            src_ref=source,
            dst_ref=target,
            send_sem=send_sem,
            recv_sem=recv_sem,
            device_id=where,
            device_id_type=MESH,
        )

    def seq_rows(seq, count=1):
        return pl.ds(pl.multiple_of(seq * row_count, row_count), count * row_count)

    barrier = pltpu.get_barrier_semaphore()
    for k in range(1, n):
        pl.semaphore_signal(
            barrier, inc=1, device_id={"attn": lax.rem(me + k, n)}, device_id_type=MESH
        )
    for k in range(1, depth):
        pl.semaphore_signal(
            barrier, inc=1, device_id={"expert": lax.rem(expert + k, depth)}, device_id_type=MESH
        )

    def norm(values, gain):
        center = jnp.mean(values, axis=-1, keepdims=True)
        spread = jnp.mean(jnp.square(values - center), axis=-1, keepdims=True)
        return ((values - center) * lax.rsqrt(spread + epsilon) * gain).astype(jnp.bfloat16)

    def norm_rows(i, carry):
        rows = pl.ds(pl.multiple_of(i * 16, 16), 16)
        result = norm(tokens_ref[rows, :].astype(jnp.float32), gain_ref[...])
        for f in range(n):
            normed[f, rows, :] = result[:, f * block : (f + 1) * block]
        return carry

    lax.fori_loop(0, row_count // 16, norm_rows, 0)
    pl.semaphore_wait(barrier, n - 1 + depth - 1)

    def piece_copy(seq):
        return send(
            normed.at[seq],
            pieces.at[seq_rows(me)],
            piece_send.at[seq],
            piece_recv.at[me],
            {"attn": seq},
        )

    def piece_arrival(seq):
        return send(
            normed.at[seq],
            pieces.at[seq_rows(seq)],
            piece_send.at[seq],
            piece_recv.at[seq],
            {"attn": seq},
        )

    for k in range(1, chips):
        piece_copy(other_chip(k) * 2 + core).start()
        piece_copy(other_chip(k) * 2 + 1 - core).start()
    piece_copy(partner).start()
    pieces[seq_rows(me), :] = normed[me]

    def pair_copy(k):
        return send(
            pair_send.at[k],
            pair_recv.at[k],
            pair_send_sem.at[k],
            pair_recv_sem.at[k],
            {"attn": partner},
        )

    def chip_copy(k):
        return send(
            chip_send.at[k],
            chip_recv.at[chip],
            chip_send_sem.at[k],
            chip_recv_sem.at[chip],
            {"attn": other_chip(k) * 2 + core},
        )

    def chip_arrival(k):
        return send(
            chip_send.at[k],
            chip_recv.at[other_chip(k)],
            chip_send_sem.at[k],
            chip_recv_sem.at[other_chip(k)],
            {"attn": other_chip(k) * 2 + core},
        )

    for k in range(chips):
        if k == 0:
            for load in loads[:3]:
                load.wait()
        else:
            piece_arrival(other_chip(k) * 2 + core).wait_recv()
        if k == 0:
            piece_arrival(partner).wait_recv()
        else:
            piece_arrival(other_chip(k) * 2 + 1 - core).wait_recv()
        rows = pieces[seq_rows(other_chip(k) * 2, 2), :]
        start = 0
        for weight in (query_all, key_all, value_all):
            size = weight.shape[1]
            partial[:, start : start + size] = jnp.dot(
                rows, weight[...], preferred_element_type=jnp.float32
            )
            start += size
        keep[k] = partial[seq_rows(core), :]
        pair_send[k] = partial[seq_rows(1 - core), :].astype(jnp.bfloat16)
        pair_copy(k).start()
        if k > 0:
            pair_copy(k).wait_recv()
            chip_send[k] = (keep[k] + pair_recv[k].astype(jnp.float32)).astype(jnp.bfloat16)
            chip_copy(k).start()
    pair_copy(0).wait_recv()
    projected[...] = keep[0] + pair_recv[0].astype(jnp.float32)
    for k in range(1, chips):
        chip_arrival(k).wait_recv()
        projected[...] = projected[...] + chip_recv[other_chip(k)].astype(jnp.float32)

    loads[3].wait()
    loads[4].wait()
    half = HD // 2
    group = query_columns // key_columns

    def turned(start):
        values = projected[:, start : start + HD]
        swapped = jnp.concatenate([values[:, half:], values[:, :half]], axis=1)
        return (values * cosine_ref[...] + swapped * sine_ref[...]).astype(jnp.bfloat16)

    score_scale = 1.0 / math.sqrt(HD)
    listed = bias_ref.shape[0]
    group_rows = group * row_count
    row_of = lax.rem(lax.broadcasted_iota(jnp.int32, (group_rows, row_count), 0), row_count)
    column_of = lax.broadcasted_iota(jnp.int32, (group_rows, row_count), 1)
    causal = row_of >= column_of
    for head in range(key_columns // HD):
        columns = slice(head * HD, (head + 1) * HD)
        queries = jnp.concatenate(
            [turned((head * group + g) * HD) for g in range(group)], axis=0
        )
        fresh_keys = turned(query_columns + head * HD)
        value_start = query_columns + key_columns + head * HD
        fresh_values = projected[:, value_start : value_start + HD].astype(jnp.bfloat16)

        def cache_rows(j):
            return slice(j * BLK, (j + 1) * BLK)

        def score(keys):
            values = lax.dot_general(
                queries, keys, TRANSPOSED, preferred_element_type=jnp.float32
            )
            return values * score_scale

        fresh_scores = jnp.where(causal, score(fresh_keys), -jnp.inf)
        scores[listed] = fresh_scores
        largest = fresh_scores
        for j in range(listed):
            block_scores = score(cache_keys[cache_rows(j), columns]) + bias_ref[j : j + 1, :]
            scores[j] = block_scores
            largest = jnp.maximum(largest, block_scores)
        largest = jnp.max(largest, axis=-1, keepdims=True)
        total = jnp.zeros((group_rows, row_count), jnp.float32)
        for j in range(listed + 1):
            exponent = jnp.exp(scores[j] - largest)
            scores[j] = exponent
            total = total + exponent
        denominator = jnp.sum(total, axis=-1, keepdims=True)
        context = jnp.zeros((group_rows, HD), jnp.float32)
        for j in range(listed + 1):
            values = fresh_values if j == listed else cache_values[cache_rows(j), columns]
            context = context + jnp.dot(
                (scores[j] / denominator).astype(jnp.bfloat16),
                values,
                preferred_element_type=jnp.float32,
            )
        for g in range(group):
            start = (head * group + g) * HD
            contexts[seq_rows(me), start : start + HD] = context[
                g * row_count : (g + 1) * row_count
            ].astype(jnp.bfloat16)

    def gather_copy(k):
        where = {"attn": partner} if k == 0 else {"attn": other_chip(k) * 2 + core}
        return send(
            contexts.at[seq_rows(me)],
            contexts.at[seq_rows(me)],
            gather_send.at[k],
            gather_recv.at[me],
            where,
        )

    def forward_copy(k):
        seq = other_chip(k) * 2 + core
        return send(
            contexts.at[seq_rows(seq)],
            contexts.at[seq_rows(seq)],
            forward_send.at[k],
            gather_recv.at[seq],
            {"attn": partner},
        )

    def gather_arrival(seq):
        return send(
            contexts.at[seq_rows(seq)],
            contexts.at[seq_rows(seq)],
            gather_send.at[0],
            gather_recv.at[seq],
            {"attn": partner},
        )

    for k in range(1, chips):
        gather_copy(k).start()
    gather_copy(0).start()

    def line_copy(k, target, rightward):
        seqs = pl.ds(other_chip(k) * 2, 2)
        return send(
            line_send.at[target, seqs],
            (from_left if rightward else from_right).at[target, seqs],
            line_send_sem.at[target, k],
            (left_sem if rightward else right_sem).at[target, k],
            {"expert": lax.rem(expert + (1 if rightward else depth - 1), depth)},
        )

    def line_add(k, target, rightward):
        seqs = pl.ds(other_chip(k) * 2, 2)
        line_copy(k, target, rightward).wait_recv()
        arrived = (from_left if rightward else from_right)[target, seqs]
        line_send[target, seqs] = (
            line_send[target, seqs].astype(jnp.float32) + arrived.astype(jnp.float32)
        ).astype(jnp.bfloat16)

    def head_sum(k):
        if k == 0:
            gather_arrival(partner).wait_recv()
            loads[5].wait()
        else:
            gather_arrival(other_chip(k) * 2 + core).wait_recv()
            forward_copy(k).start()
            gather_arrival(other_chip(k) * 2 + 1 - core).wait_recv()
        head_sums[...] = lax.dot_general(
            contexts[seq_rows(other_chip(k) * 2, 2), :],
            out_all[...],
            TRANSPOSED,
            preferred_element_type=jnp.float32,
        )
        for target in range(depth):
            for c in range(2):
                first = c * row_count + target * part_rows
                line_send[target, other_chip(k) * 2 + c] = head_sums[
                    first : first + part_rows, :
                ].astype(jnp.bfloat16)

    def line_steps(k):
        for t in range(depth - 1):
            right_target = depth - 1 - t
            left_target = t

            @pl.when(expert < right_target)
            def _():
                @pl.when(expert > 0)
                def _():
                    line_add(k, right_target, True)

                line_copy(k, right_target, True).start()

            @pl.when(expert > left_target)
            def _():
                @pl.when(expert < depth - 1)
                def _():
                    line_add(k, left_target, False)

                line_copy(k, left_target, False).start()

    def seq_copy(seq):
        return send(
            seq_send.at[seq],
            seq_recv.at[me],
            seq_send_sem.at[seq],
            seq_recv_sem.at[me],
            {"attn": seq},
        )

    def seq_arrival(seq):
        return send(
            seq_send.at[seq],
            seq_recv.at[seq],
            seq_send_sem.at[seq],
            seq_recv_sem.at[seq],
            {"attn": seq},
        )

    def line_end(k):
        seqs = pl.ds(other_chip(k) * 2, 2)

        @pl.when(expert > 0)
        def _():
            line_add(k, expert, True)

        @pl.when(expert < depth - 1)
        def _():
            line_add(k, expert, False)

        seq_send[seqs] = line_send[expert, seqs]
        if k == 0:
            seq_copy(partner).start()
            seq_recv[me] = seq_send[me]
        else:
            seq_copy(other_chip(k) * 2 + core).start()
            seq_copy(other_chip(k) * 2 + 1 - core).start()

    for k in range(chips):
        head_sum(k)
        line_steps(k)
    for k in range(chips):
        line_end(k)

    for k in range(1, n):
        seq_arrival(lax.rem(me + k, n)).wait_recv()
    my_rows = pl.ds(pl.multiple_of(expert * part_rows, part_rows), part_rows)
    for f in range(n):
        columns = slice(f * block, (f + 1) * block)
        states[expert, :, columns] = (
            tokens_ref[my_rows, columns].astype(jnp.float32) + seq_recv[f].astype(jnp.float32)
        ).astype(jnp.bfloat16)

    def state_copy(index, rightward):
        return send(
            states.at[index],
            states.at[index],
            (state_right if rightward else state_left).at[index],
            state_recv.at[index],
            {"expert": lax.rem(expert + (1 if rightward else depth - 1), depth)},
        )

    def spread(index, rightward):
        @pl.when((expert < depth - 1) if rightward else (expert > 0))
        def _():
            state_copy(index, rightward).start()

    def take(index):
        state_ref[index] = states[index]
        for i in range(0, part_rows, 16):
            rows = pl.ds(pl.multiple_of(index * part_rows + i, 16), 16)
            post[rows, :] = norm(
                states[index, i : i + 16, :].astype(jnp.float32), post_gain_ref[...]
            )

    spread(expert, True)
    spread(expert, False)
    take(expert)
    for t in range(1, depth):

        @pl.when(expert >= t)
        def _():
            state_copy(expert - t, True).wait_recv()
            spread(expert - t, True)

        @pl.when(expert + t < depth)
        def _():
            state_copy(expert + t, False).wait_recv()
            spread(expert + t, False)

        @pl.when(expert >= t)
        def _():
            take(expert - t)

        @pl.when(expert + t < depth)
        def _():
            take(expert + t)

    for start in range(0, model_width, 1024):
        columns = slice(start, start + 1024)
        buffer_ref[:, columns] = jnp.dot(
            dispatch_ref[...], post[:, columns], preferred_element_type=jnp.float32
        ).astype(jnp.bfloat16)

    for k in range(1, n):
        piece_copy(lax.rem(me + k, n)).wait_send()
        seq_copy(lax.rem(me + k, n)).wait_send()
    for k in range(chips):
        pair_copy(k).wait_send()
        gather_copy(k).wait_send()
        if k > 0:
            chip_copy(k).wait_send()
            forward_copy(k).wait_send()
        for target in range(depth):

            @pl.when(expert < target)
            def _():
                line_copy(k, target, True).wait_send()

            @pl.when(expert > target)
            def _():
                line_copy(k, target, False).wait_send()

    for index in range(depth):

        @pl.when((expert < depth - 1) & (index <= expert))
        def _():
            state_copy(index, True).wait_send()

        @pl.when((expert > 0) & (index >= expert))
        def _():
            state_copy(index, False).wait_send()


def attention_layer(
    tokens,
    norm_gain,
    cosine,
    sine,
    bias,
    post_gain,
    dispatch,
    query_weight,
    key_weight,
    value_weight,
    listed_keys,
    listed_values,
    out_weight,
):
    n = lax.axis_size("attn")
    depth = lax.axis_size("expert")
    chips = n // 2
    row_count, model_width = tokens.shape
    block = model_width // n
    query_columns = query_weight.shape[1]
    key_columns = key_weight.shape[1]
    projected = query_columns + 2 * key_columns
    part_rows = row_count // depth
    out_features = out_weight.shape[0]
    group_rows = query_columns // key_columns * row_count
    vmem = pl.BlockSpec(memory_space=pltpu.VMEM)
    anywhere = pl.BlockSpec(memory_space=pl.ANY)
    dma = pltpu.SemaphoreType.DMA
    bf16 = jnp.bfloat16
    buffer, state = pl.pallas_call(
        functools.partial(attention_kernel, chips, depth),
        out_shape=(
            jax.ShapeDtypeStruct((dispatch.shape[0], model_width), bf16),
            jax.ShapeDtypeStruct((depth, part_rows, model_width), bf16),
        ),
        in_specs=[vmem] * 7 + [anywhere] * 6,
        out_specs=(vmem, vmem),
        scratch_shapes=[
            pltpu.VMEM(query_weight.shape, bf16),
            pltpu.VMEM(key_weight.shape, bf16),
            pltpu.VMEM(value_weight.shape, bf16),
            pltpu.VMEM(listed_keys.shape, bf16),
            pltpu.VMEM(listed_values.shape, bf16),
            pltpu.VMEM(out_weight.shape, bf16),
            pltpu.VMEM((n, row_count, block), bf16),
            pltpu.VMEM((n * row_count, block), bf16),
            pltpu.VMEM((2 * row_count, projected), jnp.float32),
            pltpu.VMEM((chips, row_count, projected), jnp.float32),
            pltpu.VMEM((chips, row_count, projected), bf16),
            pltpu.VMEM((chips, row_count, projected), bf16),
            pltpu.VMEM((chips, row_count, projected), bf16),
            pltpu.VMEM((chips, row_count, projected), bf16),
            pltpu.VMEM((row_count, projected), jnp.float32),
            pltpu.VMEM((bias.shape[0] + 1, group_rows, row_count), jnp.float32),
            pltpu.VMEM((n * row_count, query_columns), bf16),
            pltpu.VMEM((2 * row_count, out_features), jnp.float32),
            pltpu.VMEM((depth, n, part_rows, out_features), bf16),
            pltpu.VMEM((depth, n, part_rows, out_features), bf16),
            pltpu.VMEM((depth, n, part_rows, out_features), bf16),
            pltpu.VMEM((n, part_rows, out_features), bf16),
            pltpu.VMEM((n, part_rows, out_features), bf16),
            pltpu.VMEM((depth, part_rows, model_width), bf16),
            pltpu.VMEM((row_count, model_width), bf16),
            dma((6,)),
            dma((n,)),
            dma((n,)),
            dma((chips,)),
            dma((chips,)),
            dma((chips,)),
            dma((chips,)),
            dma((chips,)),
            dma((chips,)),
            dma((n,)),
            dma((depth, chips)),
            dma((depth, chips)),
            dma((depth, chips)),
            dma((n,)),
            dma((n,)),
            dma((depth,)),
            dma((depth,)),
            dma((depth,)),
        ],
        compiler_params=pltpu.CompilerParams(
            collective_id=1, has_side_effects=True, vmem_limit_bytes=56 * 1024 * 1024
        ),
    )(
        tokens,
        norm_gain[None, :],
        cosine,
        sine,
        bias,
        post_gain[None, :],
        dispatch,
        query_weight,
        key_weight,
        value_weight,
        listed_keys,
        listed_values,
        out_weight,
    )
    return buffer, state.reshape(row_count, model_width)


def shards(
    tokens,
    norm_gain,
    query_weight,
    key_weight,
    value_weight,
    out_weight,
    cache_key,
    cache_value,
    block_table,
    block_count,
    expert_ids,
    gate_weights,
    post_gain,
    expert_gate,
    expert_up,
    expert_down,
):
    expert_axis_size = lax.axis_size("expert")
    expert_index = lax.axis_index("expert")
    row_count = tokens.shape[0]
    model_width = tokens.shape[1]
    share_width = model_width // expert_axis_size
    expert_total = expert_axis_size * expert_gate.shape[0]
    capacity = 3 * row_count // expert_total
    row_range = jnp.arange(row_count, dtype=jnp.int32)
    positions = (block_count[0] * BLK + row_range).astype(jnp.float32)
    half = HD // 2
    frequency = jnp.exp(
        jnp.arange(half, dtype=jnp.float32) * (-2.0 * math.log(rope_base) / HD)
    )
    angles = positions[:, None] * frequency[None, :]
    cosine = jnp.cos(angles)
    sine_part = jnp.sin(angles)
    slots = pair_slots(expert_ids, expert_total)
    slot_range = jnp.arange(capacity, dtype=jnp.int32)
    picks = [
        (expert_ids[:, pick] == expert_index)[:, None]
        & (slot_range[None, :] == slots[:, pick][:, None])
        for pick in range(2)
    ]
    listed_keys, listed_values = listed_blocks(block_table, cache_key, cache_value)
    live = jnp.arange(block_table.shape[1], dtype=jnp.int32) < block_count[0]
    bias = jnp.broadcast_to(
        jnp.where(live, 0.0, -jnp.inf).astype(jnp.float32)[:, None], (live.shape[0], BLK)
    )
    buffer, state = attention_layer(
        tokens,
        norm_gain,
        jnp.concatenate([cosine, cosine], axis=1),
        jnp.concatenate([-sine_part, sine_part], axis=1),
        bias,
        post_gain,
        (picks[0] | picks[1]).T.astype(jnp.bfloat16),
        query_weight,
        key_weight,
        value_weight,
        listed_keys,
        listed_values,
        out_weight,
    )
    state_share = lax.dynamic_slice_in_dim(state, expert_index * share_width, share_width, 1)
    mixture = expert_layer(
        buffer,
        expert_gate,
        expert_up,
        expert_down,
        jnp.stack(picks).astype(jnp.bfloat16),
        gate_weights,
    )
    return (state_share.astype(jnp.float32) + mixture).astype(jnp.bfloat16)


def solution(mesh):
    return jax.shard_map(
        shards,
        mesh=mesh,
        in_specs=(
            P(("groups", "attn"), None),
            P(),
            P("attn", "expert"),
            P("attn", "expert"),
            P("attn", "expert"),
            P("attn", "expert"),
            P(("groups", "attn"), None, "expert"),
            P(("groups", "attn"), None, "expert"),
            P(("groups", "attn"), None),
            P(("groups", "attn")),
            P(("groups", "attn"), None),
            P(("groups", "attn"), None),
            P(),
            P("expert", None, "attn"),
            P("expert", None, "attn"),
            P("expert", "attn", None),
        ),
        out_specs=P(("groups", "attn"), "expert"),
        check_vma=False,
    )
```

```python
import functools
import math

import jax
import jax.numpy as jnp
from jax import lax
from jax.experimental import pallas as pl
from jax.experimental.pallas import tpu as pltpu
from jax.sharding import PartitionSpec as P

HD = 128
BLK = 128
TILE = 256
LAG = 4
TRANSPOSED = (((1,), (1,)), ((), ()))
MESH = pl.DeviceIdType.MESH


epsilon = 1e-05
rope_base = 10000.0


def moe_kernel(
    chips,
    depth,
    buffer_ref,
    gate_ref,
    up_ref,
    down_ref,
    combine_ref,
    share_ref,
    out_ref,
    gate_all,
    up_all,
    down_all,
    piece,
    activated,
    partial,
    keep,
    pair_send,
    pair_recv,
    chip_send,
    chip_recv,
    mine,
    own_mix,
    mix_send,
    mix_recv,
    load_sem,
    gather_send,
    forward_send,
    gather_recv,
    pair_send_sem,
    pair_recv_sem,
    chip_send_sem,
    chip_recv_sem,
    mix_send_sem,
    mix_recv_sem,
):
    me = lax.axis_index("attn")
    expert = lax.axis_index("expert")
    chip = me // 2
    core = me % 2
    partner = me + 1 - 2 * core
    capacity = buffer_ref.shape[0]
    hidden = activated.shape[1]
    steps = pair_send.shape[0]
    width = partial.shape[1]
    per_owner = steps // depth
    loads = [
        pltpu.make_async_copy(source.at[0], target, load_sem.at[i])
        for i, (source, target) in enumerate(
            [(gate_ref, gate_all), (up_ref, up_all), (down_ref, down_all)]
        )
    ]
    for load in loads:
        load.start()

    def other_chip(k):
        return lax.rem(chip + k, chips)

    def other_expert(k):
        return lax.rem(expert + k, depth)

    barrier = pltpu.get_barrier_semaphore()
    pl.semaphore_signal(barrier, inc=1, device_id={"attn": partner}, device_id_type=MESH)
    for k in range(1, chips):
        pl.semaphore_signal(
            barrier, inc=1, device_id={"attn": other_chip(k) * 2 + core}, device_id_type=MESH
        )
    for k in range(1, depth):
        pl.semaphore_signal(
            barrier, inc=1, device_id={"expert": other_expert(k)}, device_id_type=MESH
        )
    pl.semaphore_wait(barrier, chips + depth - 1)

    def seq_rows(seq, count=1):
        return pl.ds(pl.multiple_of(seq * capacity, 16), count * capacity)

    def send(source, target, send_sem, recv_sem, where):
        return pltpu.make_async_remote_copy(
            src_ref=source,
            dst_ref=target,
            send_sem=send_sem,
            recv_sem=recv_sem,
            device_id=where,
            device_id_type=MESH,
        )

    def gather_copy(k):
        where = {"attn": partner} if k == 0 else {"attn": other_chip(k) * 2 + core}
        return send(
            buffer_ref, piece.at[seq_rows(me)], gather_send.at[k], gather_recv.at[me], where
        )

    def forward_copy(k):
        seq = other_chip(k) * 2 + core
        return send(
            piece.at[seq_rows(seq)],
            piece.at[seq_rows(seq)],
            forward_send.at[k],
            gather_recv.at[seq],
            {"attn": partner},
        )

    def arrival(seq):
        return send(
            buffer_ref,
            piece.at[seq_rows(seq)],
            gather_send.at[0],
            gather_recv.at[seq],
            {"attn": partner},
        )

    for k in range(1, chips):
        gather_copy(k).start()
    gather_copy(0).start()
    piece[seq_rows(me), :] = buffer_ref[...]

    def hidden_tile(rows, start, size):
        values = piece[rows, :]
        columns = pl.ds(start, size)
        gated = lax.dot_general(
            values, gate_all[columns, :], TRANSPOSED, preferred_element_type=jnp.float32
        )
        lifted = lax.dot_general(
            values, up_all[columns, :], TRANSPOSED, preferred_element_type=jnp.float32
        )
        activated[rows, columns] = (jax.nn.silu(gated) * lifted).astype(jnp.bfloat16)

    for k in range(chips):
        if k == 0:
            arrival(partner).wait_recv()
            loads[0].wait()
            loads[1].wait()
        else:
            seq = other_chip(k) * 2 + core
            arrival(seq).wait_recv()
            forward_copy(k).start()
            arrival(other_chip(k) * 2 + 1 - core).wait_recv()
        rows = seq_rows(other_chip(k) * 2, 2)
        full = hidden // TILE

        def tile_body(tile, carry):
            hidden_tile(rows, pl.multiple_of(tile * TILE, TILE), TILE)
            return carry

        lax.fori_loop(0, full, tile_body, 0)
        if hidden % TILE:
            hidden_tile(rows, full * TILE, hidden % TILE)
    loads[2].wait()

    def owner_of(step):
        return lax.rem(expert + 1 + step // per_owner, depth)

    def pair_copy(step):
        return send(
            pair_send.at[step],
            pair_recv.at[step],
            pair_send_sem.at[step],
            pair_recv_sem.at[step],
            {"attn": partner},
        )

    def chip_copy(step, k):
        return send(
            chip_send.at[step, k],
            chip_recv.at[step, chip],
            chip_send_sem.at[step, k],
            chip_recv_sem.at[step, chip],
            {"attn": other_chip(k) * 2 + core},
        )

    def chip_arrival(step, k):
        return send(
            chip_send.at[step, k],
            chip_recv.at[step, other_chip(k)],
            chip_send_sem.at[step, k],
            chip_recv_sem.at[step, other_chip(k)],
            {"attn": other_chip(k) * 2 + core},
        )

    def mix_copy(step):
        return send(
            mix_send.at[step],
            mix_recv.at[expert, lax.rem(step, per_owner)],
            mix_send_sem.at[step],
            mix_recv_sem.at[expert, lax.rem(step, per_owner)],
            {"expert": owner_of(step)},
        )

    def mix_arrival(source, part):
        return send(
            mix_send.at[0],
            mix_recv.at[source, part],
            mix_send_sem.at[0],
            mix_recv_sem.at[source, part],
            {"expert": source},
        )

    def project(step):
        columns = pl.ds(
            pl.multiple_of((owner_of(step) * per_owner + lax.rem(step, per_owner)) * width, width),
            width,
        )
        partial[...] = jnp.dot(
            activated[...], down_all[:, columns], preferred_element_type=jnp.float32
        )
        for k in range(chips):
            keep[lax.rem(step, 2), k] = partial[seq_rows(other_chip(k) * 2 + core), :]
            pair_send[step, other_chip(k)] = partial[
                seq_rows(other_chip(k) * 2 + 1 - core), :
            ].astype(jnp.bfloat16)
        pair_copy(step).start()

    def pair_sum(step):
        pair_copy(step).wait_recv()
        for k in range(chips):
            both = keep[lax.rem(step, 2), k] + pair_recv[step, other_chip(k)].astype(jnp.float32)
            if k == 0:
                mine[step] = both
            else:
                chip_send[step, k] = both.astype(jnp.bfloat16)
                chip_copy(step, k).start()

    def combine(step):
        total = mine[step]
        for k in range(1, chips):
            chip_arrival(step, k).wait_recv()
            total = total + chip_recv[step, other_chip(k)].astype(jnp.float32)
        expert_out = total.astype(jnp.bfloat16)
        mixture = lax.dot_general(
            combine_ref[...],
            expert_out,
            (((0,), (0,)), ((), ())),
            preferred_element_type=jnp.float32,
        )
        part = lax.rem(step, per_owner)

        @pl.when(step < steps - per_owner)
        def _():
            mix_send[step] = mixture.astype(jnp.bfloat16)
            mix_copy(step).start()

        @pl.when(step >= steps - per_owner)
        def _():
            own_mix[part] = mixture

    def step_body(step, carry):
        @pl.when(step < steps)
        def _():
            project(step)

        @pl.when((step >= 1) & (step <= steps))
        def _():
            pair_sum(step - 1)

        @pl.when(step >= LAG)
        def _():
            combine(step - LAG)

        return carry

    lax.fori_loop(0, steps + LAG, step_body, 0)

    for part in range(per_owner):
        columns = slice(part * width, (part + 1) * width)
        total = share_ref[:, columns].astype(jnp.float32) + own_mix[part]
        for k in range(1, depth):
            mix_arrival(other_expert(k), part).wait_recv()
            total = total + mix_recv[other_expert(k), part].astype(jnp.float32)
        out_ref[:, columns] = total.astype(jnp.bfloat16)

    for k in range(chips):
        gather_copy(k).wait_send()
    for k in range(1, chips):
        forward_copy(k).wait_send()
    def finish(step, carry):
        pair_copy(step).wait_send()
        for k in range(1, chips):
            chip_copy(step, k).wait_send()

        @pl.when(step < steps - per_owner)
        def _():
            mix_copy(step).wait_send()

        return carry

    lax.fori_loop(0, steps, finish, 0)


def expert_layer(buffer, gate, up, down, combine, share_state):
    n = lax.axis_size("attn")
    depth = lax.axis_size("expert")
    chips = n // 2
    capacity, model_width = buffer.shape
    hidden = gate.shape[2]
    row_count = share_state.shape[0]
    share = model_width // depth
    width = math.gcd(share, 512)
    per_owner = share // width
    steps = model_width // width
    vmem = pl.BlockSpec(memory_space=pltpu.VMEM)
    anywhere = pl.BlockSpec(memory_space=pl.ANY)
    dma = pltpu.SemaphoreType.DMA
    return pl.pallas_call(
        functools.partial(moe_kernel, chips, depth),
        out_shape=jax.ShapeDtypeStruct((row_count, share), jnp.bfloat16),
        in_specs=[vmem, anywhere, anywhere, anywhere, vmem, vmem],
        out_specs=vmem,
        scratch_shapes=[
            pltpu.VMEM((hidden, model_width), jnp.bfloat16),
            pltpu.VMEM((hidden, model_width), jnp.bfloat16),
            pltpu.VMEM((hidden, model_width), jnp.bfloat16),
            pltpu.VMEM((n * capacity, model_width), jnp.bfloat16),
            pltpu.VMEM((n * capacity, hidden), jnp.bfloat16),
            pltpu.VMEM((n * capacity, width), jnp.float32),
            pltpu.VMEM((2, chips, capacity, width), jnp.float32),
            pltpu.VMEM((steps, chips, capacity, width), jnp.bfloat16),
            pltpu.VMEM((steps, chips, capacity, width), jnp.bfloat16),
            pltpu.VMEM((steps, chips, capacity, width), jnp.bfloat16),
            pltpu.VMEM((steps, chips, capacity, width), jnp.bfloat16),
            pltpu.VMEM((steps, capacity, width), jnp.float32),
            pltpu.VMEM((per_owner, row_count, width), jnp.float32),
            pltpu.VMEM((steps, row_count, width), jnp.bfloat16),
            pltpu.VMEM((depth, per_owner, row_count, width), jnp.bfloat16),
            dma((3,)),
            dma((chips,)),
            dma((chips,)),
            dma((n,)),
            dma((steps,)),
            dma((steps,)),
            dma((steps, chips)),
            dma((steps, chips)),
            dma((steps,)),
            dma((depth, per_owner)),
        ],
        compiler_params=pltpu.CompilerParams(
            collective_id=0, has_side_effects=True, vmem_limit_bytes=63 * 1024 * 1024
        ),
        cost_estimate=pl.CostEstimate(
            flops=6 * n * capacity * model_width * hidden,
            bytes_accessed=6 * model_width * hidden,
            transcendentals=n * capacity * hidden,
        ),
    )(buffer, gate.swapaxes(1, 2), up.swapaxes(1, 2), down, combine, share_state)


def listed_kernel(table_ref, cache_key_ref, cache_value_ref, keys_ref, values_ref, sems):
    copies = []
    for j in range(table_ref.shape[1]):
        source = pl.ds(pl.multiple_of(table_ref[0, j] * BLK, BLK), BLK)
        target = pl.ds(j * BLK, BLK)
        for i, (cache, listed) in enumerate(
            [(cache_key_ref, keys_ref), (cache_value_ref, values_ref)]
        ):
            copies.append(
                pltpu.make_async_copy(cache.at[0, source], listed.at[target], sems.at[i, j])
            )
    for copy in copies:
        copy.start()
    for copy in copies:
        copy.wait()


def listed_blocks(block_table, cache_key, cache_value):
    listed = block_table.shape[1]
    shape = jax.ShapeDtypeStruct((listed * BLK, cache_key.shape[2]), cache_key.dtype)
    vmem = pl.BlockSpec(memory_space=pltpu.VMEM)
    anywhere = pl.BlockSpec(memory_space=pl.ANY)
    return pl.pallas_call(
        listed_kernel,
        out_shape=(shape, shape),
        in_specs=[pl.BlockSpec(memory_space=pltpu.SMEM), anywhere, anywhere],
        out_specs=(vmem, vmem),
        scratch_shapes=[pltpu.SemaphoreType.DMA((2, listed))],
    )(block_table, cache_key, cache_value)


def attention_kernel(
    chips,
    depth,
    tokens_ref,
    gain_ref,
    cosine_ref,
    sine_ref,
    bias_ref,
    post_gain_ref,
    ids_ref,
    gates_ref,
    query_weight_ref,
    key_weight_ref,
    value_weight_ref,
    cache_key_ref,
    cache_value_ref,
    out_weight_ref,
    buffer_ref,
    combine_ref,
    share_ref,
    query_all,
    key_all,
    value_all,
    cache_keys,
    cache_values,
    out_all,
    turns,
    normed,
    pieces,
    partial,
    keep,
    pair_send,
    pair_recv,
    chip_send,
    chip_recv,
    projected,
    scores,
    contexts,
    head_sums,
    line_send,
    from_left,
    from_right,
    seq_send,
    seq_recv,
    states,
    post,
    load_sem,
    piece_send,
    piece_recv,
    pair_send_sem,
    pair_recv_sem,
    chip_send_sem,
    chip_recv_sem,
    gather_send,
    forward_send,
    gather_recv,
    line_send_sem,
    left_sem,
    right_sem,
    seq_send_sem,
    seq_recv_sem,
    state_right,
    state_left,
    state_recv,
):
    me = lax.axis_index("attn")
    expert = lax.axis_index("expert")
    n = 2 * chips
    chip = me // 2
    core = me % 2
    partner = me + 1 - 2 * core
    row_count, model_width = tokens_ref.shape
    block = model_width // n
    query_columns = query_all.shape[1]
    key_columns = key_all.shape[1]
    part_rows = row_count // depth
    halves = line_send.shape[1]
    half_rows = row_count // 2
    loads = [
        pltpu.make_async_copy(source, target, load_sem.at[i])
        for i, (source, target) in enumerate(
            [
                (query_weight_ref, query_all),
                (key_weight_ref, key_all),
                (value_weight_ref, value_all),
                (cache_key_ref, cache_keys),
                (cache_value_ref, cache_values),
                (out_weight_ref, out_all),
            ]
        )
    ]
    for load in loads:
        load.start()

    def other_chip(k):
        return lax.rem(chip + k, chips)

    def send(source, target, send_sem, recv_sem, where):
        return pltpu.make_async_remote_copy(
            src_ref=source,
            dst_ref=target,
            send_sem=send_sem,
            recv_sem=recv_sem,
            device_id=where,
            device_id_type=MESH,
        )

    def seq_rows(seq, count=1):
        return pl.ds(pl.multiple_of(seq * row_count, row_count), count * row_count)

    barrier = pltpu.get_barrier_semaphore()
    for k in range(1, n):
        pl.semaphore_signal(
            barrier, inc=1, device_id={"attn": lax.rem(me + k, n)}, device_id_type=MESH
        )
    for k in range(1, depth):
        pl.semaphore_signal(
            barrier, inc=1, device_id={"expert": lax.rem(expert + k, depth)}, device_id_type=MESH
        )

    def norm(values, gain):
        center = jnp.mean(values, axis=-1, keepdims=True)
        spread = jnp.mean(jnp.square(values - center), axis=-1, keepdims=True)
        return ((values - center) * lax.rsqrt(spread + epsilon) * gain).astype(jnp.bfloat16)

    def norm_rows(i, carry):
        rows = pl.ds(pl.multiple_of(i * 16, 16), 16)
        result = norm(tokens_ref[rows, :].astype(jnp.float32), gain_ref[...])
        for f in range(n):
            normed[f, i // per_half, pl.ds(pl.multiple_of(i % per_half * 16, 16), 16), :] = result[
                :, f * block : (f + 1) * block
            ]
        return carry

    per_half = half_rows // 16

    lax.fori_loop(0, row_count // 16, norm_rows, 0)
    pl.semaphore_wait(barrier, n - 1 + depth - 1)

    def half_seq(seq, count=1):
        return pl.ds(pl.multiple_of(seq * half_rows, half_rows), count * half_rows)

    def piece_copy(seq, h):
        return send(
            normed.at[seq, h],
            pieces.at[h, half_seq(me)],
            piece_send.at[seq, h],
            piece_recv.at[me, h],
            {"attn": seq},
        )

    def piece_arrival(seq, h):
        return send(
            normed.at[seq, h],
            pieces.at[h, half_seq(seq)],
            piece_send.at[seq, h],
            piece_recv.at[seq, h],
            {"attn": seq},
        )

    for h in range(2):
        for k in range(1, chips):
            piece_copy(other_chip(k) * 2 + core, h).start()
            piece_copy(other_chip(k) * 2 + 1 - core, h).start()
        piece_copy(partner, h).start()
        pieces[h, half_seq(me), :] = normed[me, h]

    def pair_copy(k, h):
        return send(
            pair_send.at[k, h],
            pair_recv.at[k, h],
            pair_send_sem.at[k, h],
            pair_recv_sem.at[k, h],
            {"attn": partner},
        )

    def chip_copy(k, h):
        return send(
            chip_send.at[k, h],
            chip_recv.at[chip, h],
            chip_send_sem.at[k, h],
            chip_recv_sem.at[chip, h],
            {"attn": other_chip(k) * 2 + core},
        )

    def chip_arrival(k, h):
        return send(
            chip_send.at[k, h],
            chip_recv.at[other_chip(k), h],
            chip_send_sem.at[k, h],
            chip_recv_sem.at[other_chip(k), h],
            {"attn": other_chip(k) * 2 + core},
        )

    turns[0] = jnp.concatenate([cosine_ref[...], cosine_ref[...]], axis=1)
    turns[1] = jnp.concatenate([-sine_ref[...], sine_ref[...]], axis=1)
    for load in loads[:3]:
        load.wait()
    for k in range(chips):
        for h in range(2):
            if k > 0:
                piece_arrival(other_chip(k) * 2 + core, h).wait_recv()
                piece_arrival(other_chip(k) * 2 + 1 - core, h).wait_recv()
            else:
                piece_arrival(partner, h).wait_recv()
            rows = pieces[h, half_seq(other_chip(k) * 2, 2), :]
            start = 0
            for weight in (query_all, key_all, value_all):
                size = weight.shape[1]
                partial[:, start : start + size] = jnp.dot(
                    rows, weight[...], preferred_element_type=jnp.float32
                )
                start += size
            keep[k, h] = partial[half_seq(core), :]
            pair_send[k, h] = partial[half_seq(1 - core), :].astype(jnp.bfloat16)
            pair_copy(k, h).start()
            if k > 0:
                pair_copy(k, h).wait_recv()
                chip_send[k, h] = (keep[k, h] + pair_recv[k, h].astype(jnp.float32)).astype(
                    jnp.bfloat16
                )
                chip_copy(k, h).start()
    for h in range(2):
        pair_copy(0, h).wait_recv()
        total = keep[0, h] + pair_recv[0, h].astype(jnp.float32)
        for k in range(1, chips):
            chip_arrival(k, h).wait_recv()
            total = total + chip_recv[other_chip(k), h].astype(jnp.float32)
        projected[h * half_rows : (h + 1) * half_rows, :] = total

    loads[3].wait()
    loads[4].wait()
    half = HD // 2
    group = query_columns // key_columns

    def turned(start):
        values = projected[:, start : start + HD]
        swapped = jnp.concatenate([values[:, half:], values[:, :half]], axis=1)
        return (values * turns[0] + swapped * turns[1]).astype(jnp.bfloat16)

    key_heads = key_columns // HD

    def head_part(seq, head):
        width = group * HD
        return contexts.at[seq_rows(seq), pl.ds(head * width, width)]

    def gather_copy(k, head):
        where = {"attn": partner} if k == 0 else {"attn": other_chip(k) * 2 + core}
        return send(
            head_part(me, head),
            head_part(me, head),
            gather_send.at[k, head],
            gather_recv.at[me, head],
            where,
        )

    def forward_copy(k, head):
        seq = other_chip(k) * 2 + core
        return send(
            head_part(seq, head),
            head_part(seq, head),
            forward_send.at[k, head],
            gather_recv.at[seq, head],
            {"attn": partner},
        )

    def gather_arrival(seq, head):
        return send(
            head_part(seq, head),
            head_part(seq, head),
            gather_send.at[0, head],
            gather_recv.at[seq, head],
            {"attn": partner},
        )

    score_scale = 1.0 / math.sqrt(HD)
    listed = bias_ref.shape[0]
    group_rows = group * row_count
    row_of = lax.rem(lax.broadcasted_iota(jnp.int32, (group_rows, row_count), 0), row_count)
    column_of = lax.broadcasted_iota(jnp.int32, (group_rows, row_count), 1)
    causal = row_of >= column_of
    for head in range(key_columns // HD):
        columns = slice(head * HD, (head + 1) * HD)
        queries = jnp.concatenate(
            [turned((head * group + g) * HD) for g in range(group)], axis=0
        )
        fresh_keys = turned(query_columns + head * HD)
        value_start = query_columns + key_columns + head * HD
        fresh_values = projected[:, value_start : value_start + HD].astype(jnp.bfloat16)

        def cache_rows(j):
            return slice(j * BLK, (j + 1) * BLK)

        def score(keys):
            values = lax.dot_general(
                queries, keys, TRANSPOSED, preferred_element_type=jnp.float32
            )
            return values * score_scale

        fresh_scores = jnp.where(causal, score(fresh_keys), -jnp.inf)
        scores[listed] = fresh_scores
        largest = fresh_scores
        for j in range(listed):
            block_scores = score(cache_keys[cache_rows(j), columns]) + bias_ref[j : j + 1, :]
            scores[j] = block_scores
            largest = jnp.maximum(largest, block_scores)
        largest = jnp.max(largest, axis=-1, keepdims=True)
        total = jnp.zeros((group_rows, row_count), jnp.float32)
        for j in range(listed + 1):
            exponent = jnp.exp(scores[j] - largest)
            scores[j] = exponent
            total = total + exponent
        inverse = 1.0 / jnp.sum(total, axis=-1, keepdims=True)
        context = jnp.zeros((group_rows, HD), jnp.float32)
        for j in range(listed + 1):
            values = fresh_values if j == listed else cache_values[cache_rows(j), columns]
            context = context + jnp.dot(
                (scores[j] * inverse).astype(jnp.bfloat16),
                values,
                preferred_element_type=jnp.float32,
            )
        for g in range(group):
            start = (head * group + g) * HD
            contexts[seq_rows(me), start : start + HD] = context[
                g * row_count : (g + 1) * row_count
            ].astype(jnp.bfloat16)
        for k in range(1, chips):
            gather_copy(k, head).start()
        gather_copy(0, head).start()

    def line_copy(k, h, target, rightward):
        seqs = pl.ds(other_chip(k) * 2, 2)
        return send(
            line_send.at[target, h, seqs],
            (from_left if rightward else from_right).at[target, h, seqs],
            line_send_sem.at[target, k, h],
            (left_sem if rightward else right_sem).at[target, k, h],
            {"expert": lax.rem(expert + (1 if rightward else depth - 1), depth)},
        )

    def line_add(k, h, target, rightward):
        seqs = pl.ds(other_chip(k) * 2, 2)
        line_copy(k, h, target, rightward).wait_recv()
        arrived = (from_left if rightward else from_right)[target, h, seqs]
        line_send[target, h, seqs] = (
            line_send[target, h, seqs].astype(jnp.float32) + arrived.astype(jnp.float32)
        ).astype(jnp.bfloat16)

    step_rows = part_rows // halves

    def head_sum(k):
        for head in range(key_heads):
            if k == 0:
                gather_arrival(partner, head).wait_recv()
            else:
                gather_arrival(other_chip(k) * 2 + core, head).wait_recv()
                forward_copy(k, head).start()
        if k == 0:
            loads[5].wait()
        else:
            for head in range(key_heads):
                gather_arrival(other_chip(k) * 2 + 1 - core, head).wait_recv()
        head_sums[...] = lax.dot_general(
            contexts[seq_rows(other_chip(k) * 2, 2), :],
            out_all[...],
            TRANSPOSED,
            preferred_element_type=jnp.float32,
        )
        for target in range(depth):
            for h in range(halves):
                for c in range(2):
                    first = c * row_count + target * part_rows + h * step_rows
                    line_send[target, h, other_chip(k) * 2 + c] = head_sums[
                        first : first + step_rows, :
                    ].astype(jnp.bfloat16)

    def line_steps(k, h):
        for t in range(depth - 1):
            right_target = depth - 1 - t
            left_target = t

            @pl.when(expert < right_target)
            def _():
                @pl.when(expert > 0)
                def _():
                    line_add(k, h, right_target, True)

                line_copy(k, h, right_target, True).start()

            @pl.when(expert > left_target)
            def _():
                @pl.when(expert < depth - 1)
                def _():
                    line_add(k, h, left_target, False)

                line_copy(k, h, left_target, False).start()

    def seq_copy(seq, h):
        return send(
            seq_send.at[h, seq],
            seq_recv.at[h, me],
            seq_send_sem.at[h, seq],
            seq_recv_sem.at[h, me],
            {"attn": seq},
        )

    def seq_arrival(seq, h):
        return send(
            seq_send.at[h, seq],
            seq_recv.at[h, seq],
            seq_send_sem.at[h, seq],
            seq_recv_sem.at[h, seq],
            {"attn": seq},
        )

    def line_end(k, h):
        seqs = pl.ds(other_chip(k) * 2, 2)

        @pl.when(expert > 0)
        def _():
            line_add(k, h, expert, True)

        @pl.when(expert < depth - 1)
        def _():
            line_add(k, h, expert, False)

        seq_send[h, seqs] = line_send[expert, h, seqs]
        if k == 0:
            seq_copy(partner, h).start()
            seq_recv[h, me] = seq_send[h, me]
        else:
            seq_copy(other_chip(k) * 2 + core, h).start()
            seq_copy(other_chip(k) * 2 + 1 - core, h).start()

    def state_copy(index, h, rightward):
        return send(
            states.at[index, h],
            states.at[index, h],
            (state_right if rightward else state_left).at[index, h],
            state_recv.at[index, h],
            {"expert": lax.rem(expert + (1 if rightward else depth - 1), depth)},
        )

    def spread(index, h, rightward):
        @pl.when((expert < depth - 1) if rightward else (expert > 0))
        def _():
            state_copy(index, h, rightward).start()

    share = model_width // depth
    share_columns = pl.ds(pl.multiple_of(expert * share, share), share)

    def take(index, h):
        first = index * part_rows + h * step_rows
        share_ref[pl.ds(pl.multiple_of(first, 16), step_rows), :] = states[
            index, h, :, share_columns
        ]
        for i in range(0, step_rows, 16):
            rows = pl.ds(pl.multiple_of(first + i, 16), 16)
            post[rows, :] = norm(
                states[index, h, i : i + 16, :].astype(jnp.float32), post_gain_ref[...]
            )

    def make_state(h):
        for k in range(1, n):
            seq_arrival(lax.rem(me + k, n), h).wait_recv()
        first = expert * part_rows + h * step_rows
        my_rows = pl.ds(pl.multiple_of(first, 16), step_rows)
        for f in range(n):
            columns = slice(f * block, (f + 1) * block)
            states[expert, h, :, columns] = (
                tokens_ref[my_rows, columns].astype(jnp.float32)
                + seq_recv[h, f].astype(jnp.float32)
            ).astype(jnp.bfloat16)
        spread(expert, h, True)
        spread(expert, h, False)

    def hops(h):
        for t in range(1, depth):

            @pl.when(expert >= t)
            def _():
                state_copy(expert - t, h, True).wait_recv()
                spread(expert - t, h, True)

            @pl.when(expert + t < depth)
            def _():
                state_copy(expert + t, h, False).wait_recv()
                spread(expert + t, h, False)

            @pl.when(expert >= t)
            def _():
                take(expert - t, h)

            @pl.when(expert + t < depth)
            def _():
                take(expert + t, h)

    head_sum(0)
    line_steps(0, 0)
    for k in range(1, chips):
        head_sum(k)
        line_steps(k, 0)
    for k in range(chips):
        line_end(k, 0)
    for h in range(1, halves):
        for k in range(chips):
            line_steps(k, h)

    hits = [
        (ids_ref[pick : pick + 1, :] == expert).astype(jnp.float32) for pick in range(2)
    ]
    before = (
        lax.broadcasted_iota(jnp.int32, (row_count, row_count), 0)
        < lax.broadcasted_iota(jnp.int32, (row_count, row_count), 1)
    ).astype(jnp.bfloat16)
    earlier = jnp.dot(
        jnp.broadcast_to(hits[0] + hits[1], (16, row_count)).astype(jnp.bfloat16),
        before,
        preferred_element_type=jnp.float32,
    )[0:1, :]
    slot_range = lax.broadcasted_iota(jnp.int32, (buffer_ref.shape[0], row_count), 0).astype(
        jnp.float32
    )
    first_pick = jnp.where(slot_range == earlier, hits[0], 0.0)
    second_pick = jnp.where(slot_range == earlier + hits[0], hits[1], 0.0)
    dispatch = (first_pick + second_pick).astype(jnp.bfloat16)
    combine_ref[...] = (
        first_pick * gates_ref[0:1, :] + second_pick * gates_ref[1:2, :]
    ).astype(jnp.bfloat16)

    make_state(0)
    for h in range(1, halves):
        for k in range(chips):
            line_end(k, h)
    take(expert, 0)
    hops(0)
    for h in range(1, halves):
        make_state(h)
        take(expert, h)
        hops(h)

    for start in range(0, model_width, 1024):
        columns = slice(start, start + 1024)
        buffer_ref[:, columns] = jnp.dot(
            dispatch, post[:, columns], preferred_element_type=jnp.float32
        ).astype(jnp.bfloat16)

    for k in range(1, n):
        for h in range(2):
            piece_copy(lax.rem(me + k, n), h).wait_send()
        for h in range(halves):
            seq_copy(lax.rem(me + k, n), h).wait_send()
    for k in range(chips):
        for head in range(key_heads):
            gather_copy(k, head).wait_send()
            if k > 0:
                forward_copy(k, head).wait_send()
        for h in range(2):
            pair_copy(k, h).wait_send()
            if k > 0:
                chip_copy(k, h).wait_send()
        for h in range(halves):
            for target in range(depth):

                @pl.when(expert < target)
                def _():
                    line_copy(k, h, target, True).wait_send()

                @pl.when(expert > target)
                def _():
                    line_copy(k, h, target, False).wait_send()

    for h in range(halves):
        for index in range(depth):

            @pl.when((expert < depth - 1) & (index <= expert))
            def _():
                state_copy(index, h, True).wait_send()

            @pl.when((expert > 0) & (index >= expert))
            def _():
                state_copy(index, h, False).wait_send()


def attention_layer(
    tokens,
    norm_gain,
    cosine,
    sine,
    bias,
    post_gain,
    ids,
    gates,
    capacity,
    query_weight,
    key_weight,
    value_weight,
    listed_keys,
    listed_values,
    out_weight,
):
    n = lax.axis_size("attn")
    depth = lax.axis_size("expert")
    chips = n // 2
    row_count, model_width = tokens.shape
    block = model_width // n
    query_columns = query_weight.shape[1]
    key_columns = key_weight.shape[1]
    projected = query_columns + 2 * key_columns
    part_rows = row_count // depth
    out_features = out_weight.shape[0]
    halves = 2 if part_rows % 32 == 0 else 1
    step_rows = part_rows // halves
    key_heads = key_columns // HD
    group_rows = query_columns // key_columns * row_count
    vmem = pl.BlockSpec(memory_space=pltpu.VMEM)
    anywhere = pl.BlockSpec(memory_space=pl.ANY)
    dma = pltpu.SemaphoreType.DMA
    bf16 = jnp.bfloat16
    return pl.pallas_call(
        functools.partial(attention_kernel, chips, depth),
        out_shape=(
            jax.ShapeDtypeStruct((capacity, model_width), bf16),
            jax.ShapeDtypeStruct((capacity, row_count), bf16),
            jax.ShapeDtypeStruct((row_count, model_width // depth), bf16),
        ),
        in_specs=[vmem] * 8 + [anywhere] * 6,
        out_specs=(vmem, vmem, vmem),
        scratch_shapes=[
            pltpu.VMEM(query_weight.shape, bf16),
            pltpu.VMEM(key_weight.shape, bf16),
            pltpu.VMEM(value_weight.shape, bf16),
            pltpu.VMEM(listed_keys.shape, bf16),
            pltpu.VMEM(listed_values.shape, bf16),
            pltpu.VMEM(out_weight.shape, bf16),
            pltpu.VMEM((2, row_count, HD), jnp.float32),
            pltpu.VMEM((n, 2, row_count // 2, block), bf16),
            pltpu.VMEM((2, n * row_count // 2, block), bf16),
            pltpu.VMEM((row_count, projected), jnp.float32),
            pltpu.VMEM((chips, 2, row_count // 2, projected), jnp.float32),
            pltpu.VMEM((chips, 2, row_count // 2, projected), bf16),
            pltpu.VMEM((chips, 2, row_count // 2, projected), bf16),
            pltpu.VMEM((chips, 2, row_count // 2, projected), bf16),
            pltpu.VMEM((chips, 2, row_count // 2, projected), bf16),
            pltpu.VMEM((row_count, projected), jnp.float32),
            pltpu.VMEM((bias.shape[0] + 1, group_rows, row_count), jnp.float32),
            pltpu.VMEM((n * row_count, query_columns), bf16),
            pltpu.VMEM((2 * row_count, out_features), jnp.float32),
            pltpu.VMEM((depth, halves, n, step_rows, out_features), bf16),
            pltpu.VMEM((depth, halves, n, step_rows, out_features), bf16),
            pltpu.VMEM((depth, halves, n, step_rows, out_features), bf16),
            pltpu.VMEM((halves, n, step_rows, out_features), bf16),
            pltpu.VMEM((halves, n, step_rows, out_features), bf16),
            pltpu.VMEM((depth, halves, step_rows, model_width), bf16),
            pltpu.VMEM((row_count, model_width), bf16),
            dma((6,)),
            dma((n, 2)),
            dma((n, 2)),
            dma((chips, 2)),
            dma((chips, 2)),
            dma((chips, 2)),
            dma((chips, 2)),
            dma((chips, key_heads)),
            dma((chips, key_heads)),
            dma((n, key_heads)),
            dma((depth, chips, halves)),
            dma((depth, chips, halves)),
            dma((depth, chips, halves)),
            dma((halves, n)),
            dma((halves, n)),
            dma((depth, halves)),
            dma((depth, halves)),
            dma((depth, halves)),
        ],
        compiler_params=pltpu.CompilerParams(
            collective_id=1, has_side_effects=True, vmem_limit_bytes=56 * 1024 * 1024
        ),
    )(
        tokens,
        norm_gain[None, :],
        cosine,
        sine,
        bias,
        post_gain[None, :],
        ids,
        gates,
        query_weight,
        key_weight,
        value_weight,
        listed_keys,
        listed_values,
        out_weight,
    )


def shards(
    tokens,
    norm_gain,
    query_weight,
    key_weight,
    value_weight,
    out_weight,
    cache_key,
    cache_value,
    block_table,
    block_count,
    expert_ids,
    gate_weights,
    post_gain,
    expert_gate,
    expert_up,
    expert_down,
):
    row_count = tokens.shape[0]
    expert_total = lax.axis_size("expert") * expert_gate.shape[0]
    capacity = 3 * row_count // expert_total
    positions = (block_count[0] * BLK + jnp.arange(row_count, dtype=jnp.int32)).astype(jnp.float32)
    half = HD // 2
    frequency = jnp.exp(
        jnp.arange(half, dtype=jnp.float32) * (-2.0 * math.log(rope_base) / HD)
    )
    angles = positions[:, None] * frequency[None, :]
    listed_keys, listed_values = listed_blocks(block_table, cache_key, cache_value)
    block_index = lax.broadcasted_iota(jnp.int32, (block_table.shape[1], BLK), 0)
    bias = jnp.where(block_index < block_count[0], 0.0, -jnp.inf).astype(jnp.float32)
    buffer, combine, share_state = attention_layer(
        tokens,
        norm_gain,
        jnp.cos(angles),
        jnp.sin(angles),
        bias,
        post_gain,
        expert_ids.T,
        gate_weights.T,
        capacity,
        query_weight,
        key_weight,
        value_weight,
        listed_keys,
        listed_values,
        out_weight,
    )
    return expert_layer(buffer, expert_gate, expert_up, expert_down, combine, share_state)


def solution(mesh):
    return jax.shard_map(
        shards,
        mesh=mesh,
        in_specs=(
            P(("groups", "attn"), None),
            P(),
            P("attn", "expert"),
            P("attn", "expert"),
            P("attn", "expert"),
            P("attn", "expert"),
            P(("groups", "attn"), None, "expert"),
            P(("groups", "attn"), None, "expert"),
            P(("groups", "attn"), None),
            P(("groups", "attn")),
            P(("groups", "attn"), None),
            P(("groups", "attn"), None),
            P(),
            P("expert", None, "attn"),
            P("expert", None, "attn"),
            P("expert", "attn", None),
        ),
        out_specs=P(("groups", "attn"), "expert"),
        check_vma=False,
    )
```
